512 devices in a mesh: row: 16 (over z_hi, y), col: 8 (over z_lo, core), depth: 4 (over x).
Axes of the slice: x: 4, y: 8, z: 8 (z_hi: 2, z_lo: 4; z = z_hi * 4 + z_lo), core: 2. Of those that a mesh axis runs over, the one named last changes fastest.
Arguments:
- features: float32 [65536, 128], P(('row', 'col', 'depth')), may hold values from -6 to 6
- weight: float32 [128, 128], replicated, may hold values from -0.5 to 0.5
- tile_values: bfloat16 [16, 8, 4, 16, 128, 128], P('row', 'col', 'depth'), may hold values from -2 to 2
- tile_index: int32 [16, 8, 4, 16], P('row', 'col', 'depth'), may hold values from 0 to 511, as said below
- tile_counts: int32 [16, 8, 4], P('row', 'col', 'depth'), may hold values from 4 to 16, as said below
- cotangent: float32 [65536, 128], P(('row', 'col', 'depth')), may hold values from -12 to 12
Outputs:
- output: float32 [65536, 128], P(('row', 'col', 'depth'))
- weight_grad: float32 [128, 128], replicated
- feature_grad: float32 [65536, 128], P(('row', 'col', 'depth'))
The draws below stay inside these ranges and needn't reach their ends.
Inputs may be any that keep to these rules, and one draw needn't show every extreme that they name: `tile_index`: within one device the slot values are distinct; a value v places the tile at tile row v // 16 and tile column v % 16 of the device's block; only slots below tile_counts are live. `tile_counts`: some device has all 16 slots live.
All inputs are finite; a program needn't handle non-finite values.
Results may differ from the reference program's by a relative error of at most 0.0003.
Values sent between devices are 32-bit elements; how exact they have to be, the bound alone decides.
No kernel may reach another device: no remote copies, remote signals or barrier semaphores. Data moves between devices by JAX's collectives and lax.ppermute only.
A program may use at most 64 MiB of HBM per device.

```python
import math
import jax
import jax.numpy as jnp
from jax import lax

F = 128
BS = 128
PIECE = 128
NRB = 32
NCB = 16
CAP = 16
NODES = 65536
N_ROW = 16
N_COL = 8
N_DEPTH = 4
DEVICES = 512


def draw_tile_values(key, part):
    key = jax.random.fold_in(key, 5)
    key_stride, key_offset, key_extra, key_main, key_sign, key_side = jax.random.split(key, 6)
    lead = (N_ROW, N_COL, N_DEPTH, CAP)
    stride = 2 * jax.random.randint(key_stride, lead, 0, BS // 2, dtype=jnp.int32) + 1
    offset = jax.random.randint(key_offset, lead, 0, BS, dtype=jnp.int32)
    rows = jnp.arange(BS, dtype=jnp.int32)[:, None]
    cols = jnp.arange(BS, dtype=jnp.int32)[None, :]
    on_main = cols == (stride[..., None, None] * rows + offset[..., None, None]) % BS
    extra = jax.random.bernoulli(key_extra, 2.0 / BS, lead + (BS, BS))
    main_size = jax.random.uniform(key_main, lead + (BS, BS), jnp.float32, 0.5, 1.5)
    main_sign = jnp.where(jax.random.bernoulli(key_sign, 0.5, lead + (BS, BS)), 1.0, -1.0)
    side_vals = 0.7 * jax.random.truncated_normal(key_side, -3.0, 3.0, lead + (BS, BS), jnp.float32)
    values = jnp.where(on_main, main_size * main_sign, 0.0) + jnp.where(extra, side_vals, 0.0)
    return (values / jnp.sqrt(jnp.float32(CAP))).astype(jnp.bfloat16)


def draw_tile_index(key, part):
    key = jax.random.fold_in(key, 11)
    device_keys = jax.random.split(key, N_ROW * N_COL * N_DEPTH)

    def one_device(device_key):
        return jax.random.permutation(device_key, NRB * NCB)[:CAP].astype(jnp.int32)
    return jax.vmap(one_device)(device_keys).reshape(N_ROW, N_COL, N_DEPTH, CAP)


def draw_tile_counts(key, part):
    key = jax.random.fold_in(key, 23)
    key_draw, key_pick = jax.random.split(key)
    counts = jax.random.randint(key_draw, (DEVICES,), CAP // 4, CAP + 1, dtype=jnp.int32)
    chosen = jax.random.randint(key_pick, (), 0, DEVICES, dtype=jnp.int32)
    counts = jnp.where(jnp.arange(DEVICES, dtype=jnp.int32) == chosen, CAP, counts)
    return counts.reshape(N_ROW, N_COL, N_DEPTH)


def draw_cotangent(key, part):
    key = jax.random.fold_in(key, 37)
    position = jnp.arange(NODES, dtype=jnp.float32)[:, None] / NODES
    values = jax.random.truncated_normal(key, -4.0, 4.0, (NODES, F), jnp.float32) * 3.0 ** position
    return values


def steps_of(rng, extent, shards, low, high):
    level, own = 1.0, jax.random.fold_in(rng, 6)
    for axis_at, blocks in shards:
        draws = jnp.exp(jax.random.uniform(jax.random.fold_in(own, axis_at), (blocks,), jnp.float32, low / len(shards), high / len(shards)))
        level = level * jnp.repeat(draws, extent[axis_at] // blocks).reshape([-1 if axis == axis_at else 1 for axis in range(len(extent))])
    return level


def centred(key, dims, spread, limit, pieces=(), held_as=jnp.bfloat16):
    entries = spread * jax.random.normal(key, dims, jnp.float32)
    if pieces:
        entries = entries * steps_of(key, dims, pieces, -0.22, 0.18)
    return jnp.clip(entries, -limit, limit).astype(held_as)


def setup_inputs(seed: int = 0) -> dict:
    seeds = jax.random.split(jax.random.key(seed), 7)
    return {
        "features": centred(seeds[0], (NODES, F), 1.0, 6.0, ((0, 512),), jnp.float32),
        "weight": centred(seeds[1], (F, F), F ** -0.5, 0.5, (), jnp.float32),
        "tile_values": draw_tile_values(jax.random.fold_in(seeds[6], 71), 0),
        "tile_index": draw_tile_index(jax.random.fold_in(seeds[6], 71), 0),
        "tile_counts": draw_tile_counts(jax.random.fold_in(seeds[6], 71), 0),
        "cotangent": draw_cotangent(jax.random.fold_in(seeds[6], 71), 0),
    }


def forward_block(tile_data, slot_index, live_count, column_data, row_blocks, col_blocks):
    capacity = tile_data.shape[0]
    tile_size = tile_data.shape[-1]
    feat_width = column_data.shape[-1]
    block_row = slot_index // col_blocks
    block_col = slot_index % col_blocks
    picked = column_data.reshape(col_blocks, tile_size, feat_width)[block_col]
    products = jnp.einsum('tij,tjf->tif', tile_data.astype(jnp.float32), picked, precision=lax.Precision.HIGHEST)
    active = jnp.arange(capacity, dtype=jnp.int32) < live_count
    selector = ((block_row[None, :] == jnp.arange(row_blocks, dtype=jnp.int32)[:, None]) & active[None, :]).astype(jnp.float32)
    summed = jnp.dot(selector, products.reshape(capacity, tile_size * feat_width), precision=lax.Precision.HIGHEST, preferred_element_type=jnp.float32)
    return summed.reshape(row_blocks * tile_size, feat_width)

def backward_block(tile_data, slot_index, live_count, slab_data, row_blocks, col_blocks):
    capacity = tile_data.shape[0]
    tile_size = tile_data.shape[-1]
    feat_width = slab_data.shape[-1]
    block_row = slot_index // col_blocks
    block_col = slot_index % col_blocks
    picked = slab_data.reshape(row_blocks, tile_size, feat_width)[block_row]
    products = jnp.einsum('tji,tjf->tif', tile_data.astype(jnp.float32), picked, precision=lax.Precision.HIGHEST)
    active = jnp.arange(capacity, dtype=jnp.int32) < live_count
    selector = ((block_col[None, :] == jnp.arange(col_blocks, dtype=jnp.int32)[:, None]) & active[None, :]).astype(jnp.float32)
    summed = jnp.dot(selector, products.reshape(capacity, tile_size * feat_width), precision=lax.Precision.HIGHEST, preferred_element_type=jnp.float32)
    return summed.reshape(col_blocks * tile_size, feat_width)

def reference(features, weight, tile_values, tile_index, tile_counts, cotangent):
    groups = N_COL * N_DEPTH
    tile_grid = tile_values.reshape(N_ROW, groups, CAP, BS, BS)
    index_grid = tile_index.reshape(N_ROW, groups, CAP)
    count_grid = tile_counts.reshape(N_ROW, groups)
    feature_grid = features.reshape(N_ROW, groups, PIECE, F)

    def slab_forward(row_pos):

        def add_group(running, group_pos):
            column_data = feature_grid[:, group_pos].reshape(N_ROW * PIECE, F)
            term = forward_block(tile_grid[row_pos, group_pos], index_grid[row_pos, group_pos], count_grid[row_pos, group_pos], column_data, NRB, NCB)
            return (running + term, None)
        running, _ = lax.scan(add_group, jnp.zeros((NRB * BS, F), jnp.float32), jnp.arange(groups, dtype=jnp.int32))
        return running
    aggregated = lax.map(slab_forward, jnp.arange(N_ROW, dtype=jnp.int32)).reshape(NODES, F)
    pre_act = jnp.dot(aggregated, weight, precision=lax.Precision.HIGHEST, preferred_element_type=jnp.float32)
    sigma_pre = jax.nn.sigmoid(pre_act)
    output = pre_act * sigma_pre
    pre_grad = cotangent * sigma_pre * (1.0 + pre_act * (1.0 - sigma_pre))
    weight_grad = jnp.dot(aggregated.T, pre_grad, precision=lax.Precision.HIGHEST, preferred_element_type=jnp.float32) / math.sqrt(NODES)
    mixed = jnp.dot(pre_grad, weight.T, precision=lax.Precision.HIGHEST, preferred_element_type=jnp.float32)
    mixed_grid = mixed.reshape(N_ROW, groups * PIECE, F)

    def group_backward(group_pos):

        def add_row(running, row_pos):
            term = backward_block(tile_grid[row_pos, group_pos], index_grid[row_pos, group_pos], count_grid[row_pos, group_pos], mixed_grid[row_pos], NRB, NCB)
            return (running + term, None)
        running, _ = lax.scan(add_row, jnp.zeros((NCB * BS, F), jnp.float32), jnp.arange(N_ROW, dtype=jnp.int32))
        return running
    column_parts = lax.map(group_backward, jnp.arange(groups, dtype=jnp.int32))
    feature_grad = column_parts.reshape(groups, N_ROW, PIECE, F).transpose(1, 0, 2, 3).reshape(NODES, F)
    return (output, weight_grad, feature_grad)
```

```python
import functools
import math

import jax
import jax.numpy as jnp
from jax import lax
from jax.experimental import pallas as pl
from jax.experimental.pallas import tpu as pltpu
from jax.sharding import PartitionSpec as P

MEM = 48 * 1024 * 1024


def split_bf16(value):
    high = value.astype(jnp.bfloat16)
    low = (value - high.astype(jnp.float32)).astype(jnp.bfloat16)
    return high, low


def dot3(left, right, dims):
    lh, ll = split_bf16(left)
    rh, rl = split_bf16(right)

    def one(a, b):
        return lax.dot_general(a, b, (dims, ((), ())), preferred_element_type=jnp.float32)

    return one(lh, rh) + (one(lh, rl) + one(ll, rh))


def half_place(block, inner):
    return (block // inner) % 2, (block // (2 * inner)) * inner + block % inner


def forward_kernel(inner, index_ref, count_ref, tiles_ref, cols_ref, keep_ref, send_ref, acc, sems):
    capacity = tiles_ref.shape[0]
    col_blocks = cols_ref.shape[0]
    core = lax.axis_index("col") % 2
    acc[...] = jnp.zeros_like(acc)
    for slot in range(capacity):
        place = index_ref[slot]
        row, col = place // col_blocks, place % col_blocks
        half, spot = half_place(row, inner)
        data = jnp.where(slot < count_ref[0], cols_ref[col], 0.0)
        high, low = split_bf16(data)
        tile = tiles_ref[slot]
        product = jnp.dot(
            jnp.concatenate([tile, tile], axis=1),
            jnp.concatenate([high, low], axis=0),
            preferred_element_type=jnp.float32,
        )
        other = (half + core) % 2
        acc[other, spot] = acc[other, spot] + product
    out = [
        pltpu.make_async_copy(acc.at[1], send_ref, sems.at[1]),
        pltpu.make_async_copy(acc.at[0], keep_ref, sems.at[0]),
    ]
    for copy in out:
        copy.start()
    for copy in out:
        copy.wait()


def middle_kernel(parts_ref, weight_ref, cot_ref, output_ref, packet_ref):
    peers = parts_ref.shape[0]
    total = parts_ref[0]
    for peer in range(1, peers):
        total = total + parts_ref[peer]
    weight = weight_ref[...]
    pre = dot3(total, weight, ((1,), (0,)))
    sig = jax.nn.sigmoid(pre)
    output_ref[...] = pre * sig
    grad = cot_ref[...] * sig * (1.0 + pre * (1.0 - sig))
    moving = dot3(grad, weight, ((1,), (1,)))
    term = dot3(total, grad, ((0,), (0,)))
    size = moving.shape[0]
    share = packet_ref.shape[1] - size
    for peer in range(peers):
        packet_ref[peer, 0:size] = moving
        packet_ref[peer, size : size + share] = term[peer * share : (peer + 1) * share]


def backward_kernel(inner, index_ref, count_ref, tiles_ref, own_ref, other_ref, packet_ref):
    capacity, size = tiles_ref.shape[0], tiles_ref.shape[1]
    col_blocks = packet_ref.shape[0]
    share = packet_ref.shape[1] - size
    core = lax.axis_index("col") % 2
    packet_ref[:, 0:size] = jnp.zeros((col_blocks, size, packet_ref.shape[2]), jnp.float32)
    term = own_ref[0, size : size + share] + other_ref[0, size : size + share]
    for peer in range(1, own_ref.shape[0]):
        term = term + (own_ref[peer, size : size + share] + other_ref[peer, size : size + share])
    for block in range(col_blocks):
        packet_ref[block, size : size + share] = term
    for slot in range(capacity):
        place = index_ref[slot]
        row, col = place // col_blocks, place % col_blocks
        half, spot = half_place(row, inner)
        data = jnp.where(half == core, own_ref[spot, 0:size], other_ref[spot, 0:size])
        data = jnp.where(slot < count_ref[0], data, 0.0)
        high, low = split_bf16(data)
        tile = tiles_ref[slot]
        product = lax.dot_general(
            jnp.concatenate([tile, tile], axis=0),
            jnp.concatenate([high, low], axis=0),
            (((0,), (0,)), ((), ())),
            preferred_element_type=jnp.float32,
        )
        packet_ref[col, 0:size] = packet_ref[col, 0:size] + product


def on_device(features, weight, tile_values, tile_index, tile_counts, cotangent):
    tiles = tile_values.reshape(tile_values.shape[-3:])
    slot_index = tile_index.reshape(-1)
    live_count = tile_counts.reshape(-1)
    capacity, size, _ = tiles.shape
    width = features.shape[1]
    rows = lax.axis_size("row")
    cols = lax.axis_size("col")
    inner = lax.axis_size("depth")
    half = cols * inner // 2
    share = size // half
    node_total = size * rows * cols * inner
    swap = [(i, i ^ 1) for i in range(cols)]
    same_core = [[(z * 2 + c) * inner + x for z in range(cols // 2) for x in range(inner)] for c in range(2)]
    params = pltpu.CompilerParams(vmem_limit_bytes=MEM)
    smem = pl.BlockSpec(memory_space=pltpu.SMEM)
    vmem = pl.BlockSpec(memory_space=pltpu.VMEM)
    hbm = pl.BlockSpec(memory_space=pl.ANY)

    def swap_half(value):
        return lax.all_to_all(
            value, ("col", "depth"), 0, 0, tiled=True, axis_index_groups=same_core
        )

    spread = jnp.broadcast_to(features[None], (rows,) + features.shape)
    column_data = lax.all_to_all(spread, "row", 0, 0, tiled=True)
    block = jax.ShapeDtypeStruct((half, size, width), jnp.float32)
    keep, send = pl.pallas_call(
        functools.partial(forward_kernel, inner),
        out_shape=(block, block),
        in_specs=[smem, smem, vmem, vmem],
        out_specs=(hbm, hbm),
        scratch_shapes=[
            pltpu.VMEM((2, half, size, width), jnp.float32),
            pltpu.SemaphoreType.DMA((2,)),
        ],
        compiler_params=params,
        name="forward_tiles",
    )(slot_index, live_count, tiles, column_data)
    partial = keep + lax.ppermute(send, "col", swap)
    parts = swap_half(partial)
    output, packet = pl.pallas_call(
        middle_kernel,
        out_shape=(
            jax.ShapeDtypeStruct((size, width), jnp.float32),
            jax.ShapeDtypeStruct((half, size + share, width), jnp.float32),
        ),
        in_specs=[vmem, vmem, vmem],
        out_specs=(vmem, vmem),
        compiler_params=params,
        name="dense_layer",
    )(parts, weight, cotangent)
    own = swap_half(packet)
    other = lax.ppermute(own, "col", swap)
    back = pl.pallas_call(
        functools.partial(backward_kernel, inner),
        out_shape=jax.ShapeDtypeStruct((rows, size + share, width), jnp.float32),
        in_specs=[smem, smem, vmem, vmem, vmem],
        out_specs=vmem,
        compiler_params=params,
        name="backward_tiles",
    )(slot_index, live_count, tiles, own, other)
    landed = lax.all_to_all(back, "row", 0, 0, tiled=True)
    summed = landed.sum(axis=0)
    feature_grad = summed[:size]
    term = summed[size:] * (1.0 / math.sqrt(node_total))
    weight_grad = swap_half(jnp.broadcast_to(term[None], (half, share, width))).reshape(half * share, width)
    return (output, weight_grad, feature_grad)


def solution(mesh):
    return jax.shard_map(
        on_device,
        mesh=mesh,
        in_specs=(
            P(("row", "col", "depth"), None),
            P(),
            P("row", "col", "depth", None, None, None),
            P("row", "col", "depth", None),
            P("row", "col", "depth"),
            P(("row", "col", "depth"), None),
        ),
        out_specs=(P(("row", "col", "depth"), None), P(), P(("row", "col", "depth"), None)),
        check_vma=False,
    )
```

```python
import functools
import math

import jax
import jax.numpy as jnp
from jax import lax
from jax.experimental import pallas as pl
from jax.experimental.pallas import tpu as pltpu
from jax.sharding import PartitionSpec as P

MEM = 48 * 1024 * 1024
MIX = True
CD = ("col", "depth")


def split_bf16(value):
    high = value.astype(jnp.bfloat16)
    low = (value - high.astype(jnp.float32)).astype(jnp.bfloat16)
    return high, low


def dot3(left, right, dims):
    lh, ll = split_bf16(left)
    rh, rl = split_bf16(right)

    def one(a, b):
        return lax.dot_general(a, b, (dims, ((), ())), preferred_element_type=jnp.float32)

    return one(lh, rh) + (one(lh, rl) + one(ll, rh))


def half_place(block, inner, outer):
    half, run, step = (block // inner) % 2, block // (2 * inner), block % inner
    depth_first = step * outer + run
    if MIX:
        return half, jnp.where(half == 0, depth_first, run * inner + step)
    return half, depth_first


def tile_product(tile, data, transposed):
    high, low = split_bf16(data)
    axis = 0 if transposed else 1
    return lax.dot_general(
        jnp.concatenate([tile, tile], axis=axis),
        jnp.concatenate([high, low], axis=0),
        (((axis,), (0,)), ((), ())),
        preferred_element_type=jnp.float32,
    )


def spread_kernel(features_ref, spread_ref):
    data = features_ref[...]
    for peer in range(spread_ref.shape[0]):
        spread_ref[peer] = data


def forward_kernel(inner, outer, index_ref, count_ref, tiles_ref, cols_ref, keep_ref, send_ref, acc, sems):
    core = lax.axis_index("col") % 2
    blocks = cols_ref.shape[0]
    acc[...] = jnp.zeros_like(acc)
    for slot in range(tiles_ref.shape[0]):
        place = index_ref[slot]
        half, spot = half_place(place // blocks, inner, outer)
        data = jnp.where(slot < count_ref[0], cols_ref[place % blocks], 0.0)
        away = (half + core) % 2
        acc[away, spot] = acc[away, spot] + tile_product(tiles_ref[slot], data, False)
    out = [
        pltpu.make_async_copy(acc.at[1], send_ref, sems.at[1]),
        pltpu.make_async_copy(acc.at[0], keep_ref, sems.at[0]),
    ]
    for copy in out:
        copy.start()
    for copy in out:
        copy.wait()


def middle_kernel(inner, parts_ref, weight_ref, cot_ref, output_ref, packet_ref):
    core = lax.axis_index("col") % 2
    total = parts_ref[0]
    for peer in range(1, parts_ref.shape[0]):
        total = total + parts_ref[peer]
    weight = weight_ref[...]
    pre = dot3(total, weight, ((1,), (0,)))
    sig = jax.nn.sigmoid(pre)
    output_ref[...] = pre * sig
    grad = cot_ref[...] * sig * (1.0 + pre * (1.0 - sig))
    moving = dot3(grad, weight, ((1,), (1,)))
    term = dot3(total, grad, ((0,), (0,)))
    size = moving.shape[0]
    peers = packet_ref.shape[0]
    rows = size // (peers * inner)
    for peer in range(peers):
        packet_ref[peer, 0:size] = moving
        for step in range(inner):
            at = (peer * inner + step) * rows
            piece = term[at : at + rows]
            if MIX:
                at = (step * inner + peer) * rows
                piece = jnp.where(core == 0, piece, term[at : at + rows])
            packet_ref[peer, size + step * rows : size + (step + 1) * rows] = piece


def repack_kernel(landed_ref, packet_ref):
    outer, length = landed_ref.shape[0], landed_ref.shape[1]
    part, size = packet_ref.shape[1], landed_ref.shape[2]
    term = landed_ref[0, size:length]
    for peer in range(1, outer):
        term = term + landed_ref[peer, size:length]
    share = part - outer * size
    for peer in range(packet_ref.shape[0]):
        for piece in range(outer):
            packet_ref[peer, piece * size : (piece + 1) * size] = landed_ref[piece, 0:size]
        packet_ref[peer, outer * size : part] = term[peer * share : (peer + 1) * share]


def backward_kernel(inner, outer, index_ref, count_ref, tiles_ref, own_ref, other_ref, packet_ref):
    blocks = packet_ref.shape[0]
    size = tiles_ref.shape[1]
    core = lax.axis_index("col") % 2
    span = outer * size
    share = own_ref.shape[1] - span
    term = own_ref[0, span:] + other_ref[0, span:]
    for peer in range(1, own_ref.shape[0]):
        term = term + (own_ref[peer, span:] + other_ref[peer, span:])
    for block in range(blocks):
        packet_ref[block, 0:size] = jnp.zeros((size, packet_ref.shape[2]), jnp.float32)
        packet_ref[block, size : size + share] = term
    for slot in range(tiles_ref.shape[0]):
        place = index_ref[slot]
        col = place % blocks
        half, spot = half_place(place // blocks, inner, outer)
        at = pl.ds(pl.multiple_of((spot % outer) * size, size), size)
        data = jnp.where(half == core, own_ref[spot // outer, at], other_ref[spot // outer, at])
        data = jnp.where(slot < count_ref[0], data, 0.0)
        packet_ref[col, 0:size] = packet_ref[col, 0:size] + tile_product(tiles_ref[slot], data, True)


def last_kernel(scale, landed_ref, grad_ref, spread_ref):
    size = grad_ref.shape[0]
    total = landed_ref[0]
    for peer in range(1, landed_ref.shape[0]):
        total = total + landed_ref[peer]
    grad_ref[...] = total[0:size]
    for peer in range(spread_ref.shape[0]):
        spread_ref[peer] = total[size:] * scale


def on_device(features, weight, tile_values, tile_index, tile_counts, cotangent):
    tiles = tile_values.reshape(tile_values.shape[-3:])
    slot_index = tile_index.reshape(-1)
    live_count = tile_counts.reshape(-1)
    size, width = features.shape
    rows = lax.axis_size("row")
    cols = lax.axis_size("col")
    inner = lax.axis_size("depth")
    outer = cols // 2
    assert inner == outer
    half = outer * inner
    share = size // half
    node_total = size * rows * cols * inner
    swap = [(i, i ^ 1) for i in range(cols)]
    place = lambda z, c, x: (z * 2 + c) * inner + x
    along_depth = [[[place(z, c, x) for x in range(inner)] for z in range(outer)] for c in range(2)]
    along_col = [[[place(z, c, x) for z in range(outer)] for x in range(inner)] for c in range(2)]
    if MIX:
        large, small = along_depth[0] + along_col[1], along_col[0] + along_depth[1]
    else:
        large, small = along_depth[0] + along_depth[1], along_col[0] + along_col[1]
    same_core = [[place(z, c, x) for z in range(outer) for x in range(inner)] for c in range(2)]
    smem = pl.BlockSpec(memory_space=pltpu.SMEM)
    vmem = pl.BlockSpec(memory_space=pltpu.VMEM)
    hbm = pl.BlockSpec(memory_space=pl.ANY)

    def shape(*dims):
        return jax.ShapeDtypeStruct(dims + (width,), jnp.float32)

    def call(kernel, name, out_shape, in_specs, out_specs, scratch=()):
        return pl.pallas_call(
            kernel,
            out_shape=out_shape,
            in_specs=in_specs,
            out_specs=out_specs,
            scratch_shapes=scratch,
            compiler_params=pltpu.CompilerParams(vmem_limit_bytes=MEM),
            name=name,
        )

    def exchange(value, groups):
        return lax.all_to_all(value, CD, 0, 0, tiled=True, axis_index_groups=groups)

    spread = call(spread_kernel, "spread", shape(rows, size), [vmem], vmem)(features)
    columns = lax.all_to_all(spread, "row", 0, 0, tiled=True)
    keep, send = call(
        functools.partial(forward_kernel, inner, outer),
        "forward_tiles",
        (shape(half, size), shape(half, size)),
        [smem, smem, vmem, vmem],
        (hbm, hbm),
        [pltpu.VMEM((2, half, size, width), jnp.float32), pltpu.SemaphoreType.DMA((2,))],
    )(slot_index, live_count, tiles, columns)
    parts = keep + lax.ppermute(send, "col", swap)
    landed = exchange(parts.reshape(inner, outer * size, width), large)
    parts = exchange(landed.sum(axis=0).reshape(outer, size, width), small)
    output, packet = call(
        functools.partial(middle_kernel, inner),
        "dense_layer",
        (shape(size), shape(outer, size + size // outer)),
        [vmem, vmem, vmem],
        (vmem, vmem),
    )(parts, weight, cotangent)
    landed = exchange(packet, small)
    packet = call(repack_kernel, "repack", shape(inner, outer * size + share), [vmem], vmem)(landed)
    own = exchange(packet, large)
    other = lax.ppermute(own, "col", swap)
    back = call(
        functools.partial(backward_kernel, inner, outer),
        "backward_tiles",
        shape(rows, size + share),
        [smem, smem, vmem, vmem, vmem],
        vmem,
    )(slot_index, live_count, tiles, own, other)
    landed = lax.all_to_all(back, "row", 0, 0, tiled=True)
    feature_grad, spread = call(
        functools.partial(last_kernel, 1.0 / math.sqrt(node_total)),
        "add_landed",
        (shape(size), shape(half, share)),
        [vmem],
        (vmem, vmem),
    )(landed)
    weight_grad = exchange(spread, same_core).reshape(size, width)
    return (output, weight_grad, feature_grad)


def solution(mesh):
    return jax.shard_map(
        on_device,
        mesh=mesh,
        in_specs=(
            P(("row", "col", "depth"), None),
            P(),
            P("row", "col", "depth", None, None, None),
            P("row", "col", "depth", None),
            P("row", "col", "depth"),
            P(("row", "col", "depth"), None),
        ),
        out_specs=(P(("row", "col", "depth"), None), P(), P(("row", "col", "depth"), None)),
        check_vma=False,
    )
```

```python
import functools
import math

import jax
import jax.numpy as jnp
from jax import lax
from jax.experimental import pallas as pl
from jax.experimental.pallas import tpu as pltpu
from jax.sharding import PartitionSpec as P

MEM = 48 * 1024 * 1024
TURN = 8
ZFAST = True
CD = ("col", "depth")


def split_bf16(value):
    high = value.astype(jnp.bfloat16)
    low = (value - high.astype(jnp.float32)).astype(jnp.bfloat16)
    return high, low


def dot3(left, right, dims):
    lh, ll = split_bf16(left)
    rh, rl = split_bf16(right)

    def one(a, b):
        return lax.dot_general(a, b, (dims, ((), ())), preferred_element_type=jnp.float32)

    return one(lh, rh) + (one(lh, rl) + one(ll, rh))


def half_place(block, inner, outer):
    half, run, step = (block // inner) % 2, block // (2 * inner), block % inner
    depth_first = step * outer + run
    return half, jnp.where(half == 0, depth_first, run * inner + step)


def tile_product(tile, data, transposed):
    high, low = split_bf16(data)
    axis = 0 if transposed else 1
    return lax.dot_general(
        jnp.concatenate([tile, tile], axis=axis),
        jnp.concatenate([high, low], axis=0),
        (((axis,), (0,)), ((), ())),
        preferred_element_type=jnp.float32,
    )


def parity_place(block):
    if ZFAST:
        return block % 2, ((block % TURN) // 2) * 2 + block // TURN
    return block % 2, (block // TURN) * (TURN // 2) + (block % TURN) // 2


def forward_kernel(inner, outer, blocks, index_ref, count_ref, tiles_ref, near_ref, far_ref, keep_ref, send_ref):
    core = lax.axis_index("col") % 2
    mine = lax.axis_index("row") % 2
    keep_ref[...] = jnp.zeros_like(keep_ref)
    send_ref[...] = jnp.zeros_like(send_ref)
    for slot in range(tiles_ref.shape[0]):
        place = index_ref[slot]
        half, spot = half_place(place // blocks, inner, outer)
        parity, at = parity_place(place % blocks)
        data = jnp.where(parity == mine, near_ref[at], far_ref[at])
        data = jnp.where(slot < count_ref[0], data, 0.0)
        product = tile_product(tiles_ref[slot], data, False)
        kept = half == core
        keep_ref[spot] = keep_ref[spot] + jnp.where(kept, product, 0.0)
        send_ref[spot] = send_ref[spot] + jnp.where(kept, 0.0, product)


def middle_kernel(inner, parts_ref, weight_ref, cot_ref, output_ref, packet_ref):
    core = lax.axis_index("col") % 2
    total = parts_ref[0]
    for peer in range(1, parts_ref.shape[0]):
        total = total + parts_ref[peer]
    weight = weight_ref[...]
    pre = dot3(total, weight, ((1,), (0,)))
    sig = jax.nn.sigmoid(pre)
    output_ref[...] = pre * sig
    grad = cot_ref[...] * sig * (1.0 + pre * (1.0 - sig))
    moving = dot3(grad, weight, ((1,), (1,)))
    term = dot3(total, grad, ((0,), (0,)))
    size = moving.shape[0]
    peers = packet_ref.shape[0]
    rows = size // (peers * inner)
    for peer in range(peers):
        packet_ref[peer, 0:size] = moving
        for step in range(inner):
            at = (peer * inner + step) * rows
            piece = term[at : at + rows]
            at = (step * inner + peer) * rows
            piece = jnp.where(core == 0, piece, term[at : at + rows])
            packet_ref[peer, size + step * rows : size + (step + 1) * rows] = piece


def repack_kernel(landed_ref, packet_ref):
    outer, length = landed_ref.shape[0], landed_ref.shape[1]
    part, size = packet_ref.shape[1], landed_ref.shape[2]
    term = landed_ref[0, size:length]
    for peer in range(1, outer):
        term = term + landed_ref[peer, size:length]
    share = part - outer * size
    for peer in range(packet_ref.shape[0]):
        for piece in range(outer):
            packet_ref[peer, piece * size : (piece + 1) * size] = landed_ref[piece, 0:size]
        packet_ref[peer, outer * size : part] = term[peer * share : (peer + 1) * share]


def backward_kernel(
    inner, outer, blocks, index_ref, count_ref, tiles_ref, own_ref, other_ref, keep_ref, away_ref
):
    size = tiles_ref.shape[1]
    core = lax.axis_index("col") % 2
    mine = lax.axis_index("row") % 2
    span = outer * size
    term = own_ref[0, span:] + other_ref[0, span:]
    for peer in range(1, own_ref.shape[0]):
        term = term + (own_ref[peer, span:] + other_ref[peer, span:])
    zero = jnp.zeros((size, keep_ref.shape[2]), jnp.float32)
    for block in range(keep_ref.shape[0]):
        for ref in (keep_ref, away_ref):
            ref[block, 0:size] = zero
            ref[block, size:] = term
    for slot in range(tiles_ref.shape[0]):
        place = index_ref[slot]
        half, spot = half_place(place // blocks, inner, outer)
        parity, to = parity_place(place % blocks)
        at = pl.ds(pl.multiple_of((spot % outer) * size, size), size)
        data = jnp.where(half == core, own_ref[spot // outer, at], other_ref[spot // outer, at])
        data = jnp.where(slot < count_ref[0], data, 0.0)
        product = tile_product(tiles_ref[slot], data, True)
        kept = parity == mine
        keep_ref[to, 0:size] = keep_ref[to, 0:size] + jnp.where(kept, product, 0.0)
        away_ref[to, 0:size] = away_ref[to, 0:size] + jnp.where(kept, 0.0, product)


def last_kernel(scale, landed_ref, grad_ref, spread_ref):
    size = grad_ref.shape[0]
    total = landed_ref[0]
    for peer in range(1, landed_ref.shape[0]):
        total = total + landed_ref[peer]
    grad_ref[...] = total[0:size]
    for peer in range(spread_ref.shape[0]):
        spread_ref[peer] = total[size:] * scale


def on_device(features, weight, tile_values, tile_index, tile_counts, cotangent):
    tiles = tile_values.reshape(tile_values.shape[-3:])
    slot_index = tile_index.reshape(-1)
    live_count = tile_counts.reshape(-1)
    size, width = features.shape
    rows = lax.axis_size("row")
    cols = lax.axis_size("col")
    inner = lax.axis_size("depth")
    outer = cols // 2
    assert inner == outer
    half = outer * inner
    share = size // half
    node_total = size * rows * cols * inner
    swap = [(i, i ^ 1) for i in range(cols)]
    place = lambda z, c, x: (z * 2 + c) * inner + x
    along_depth = [[[place(z, c, x) for x in range(inner)] for z in range(outer)] for c in range(2)]
    along_col = [[[place(z, c, x) for z in range(outer)] for x in range(inner)] for c in range(2)]
    large, small = along_depth[0] + along_col[1], along_col[0] + along_depth[1]
    def beside(row, core):
        base, y = row - row % TURN, row % TURN
        return base + (y + (1 if (y + core) % 2 == 0 else -1)) % TURN

    if ZFAST:
        same_parity = [[z + y for y in range(p, TURN, 2) for z in range(0, rows, TURN)] for p in range(2)]
    else:
        same_parity = [[z + y for z in range(0, rows, TURN) for y in range(p, TURN, 2)] for p in range(2)]
    neighbour = [(y * cols + c, beside(y, c % 2) * cols + c) for y in range(rows) for c in range(cols)]
    same_core = [[place(z, c, x) for z in range(outer) for x in range(inner)] for c in range(2)]
    smem = pl.BlockSpec(memory_space=pltpu.SMEM)
    vmem = pl.BlockSpec(memory_space=pltpu.VMEM)

    def shape(*dims):
        return jax.ShapeDtypeStruct(dims + (width,), jnp.float32)

    def call(kernel, name, out_shape, in_specs, out_specs, scratch=()):
        return pl.pallas_call(
            kernel,
            out_shape=out_shape,
            in_specs=in_specs,
            out_specs=out_specs,
            scratch_shapes=scratch,
            compiler_params=pltpu.CompilerParams(vmem_limit_bytes=MEM),
            name=name,
        )

    def exchange(value, groups):
        return lax.all_to_all(value, CD, 0, 0, tiled=True, axis_index_groups=groups)

    spread = jnp.broadcast_to(features[None], (rows // 2, size, width))
    near = lax.all_to_all(spread, "row", 0, 0, tiled=True, axis_index_groups=same_parity)
    far = lax.ppermute(near, ("row", "col"), neighbour)
    keep, send = call(
        functools.partial(forward_kernel, inner, outer, rows),
        "forward_tiles",
        (shape(half, size), shape(half, size)),
        [smem, smem, vmem, vmem, vmem],
        (vmem, vmem),
    )(slot_index, live_count, tiles, near, far)
    parts = keep + lax.ppermute(send, "col", swap)
    landed = exchange(parts.reshape(inner, outer * size, width), large)
    parts = exchange(landed.sum(axis=0).reshape(outer, size, width), small)
    output, packet = call(
        functools.partial(middle_kernel, inner),
        "dense_layer",
        (shape(size), shape(outer, size + size // outer)),
        [vmem, vmem, vmem],
        (vmem, vmem),
    )(parts, weight, cotangent)
    landed = exchange(packet, small)
    packet = call(repack_kernel, "repack", shape(inner, outer * size + share), [vmem], vmem)(landed)
    own = exchange(packet, large)
    other = lax.ppermute(own, "col", swap)
    keep, away = call(
        functools.partial(backward_kernel, inner, outer, rows),
        "backward_tiles",
        (shape(rows // 2, size + share),) * 2,
        [smem, smem, vmem, vmem, vmem],
        (vmem, vmem),
    )(slot_index, live_count, tiles, own, other)
    moved = keep + lax.ppermute(away, ("row", "col"), neighbour)
    landed = lax.all_to_all(moved, "row", 0, 0, tiled=True, axis_index_groups=same_parity)
    feature_grad, spread = call(
        functools.partial(last_kernel, 1.0 / math.sqrt(node_total)),
        "add_landed",
        (shape(size), shape(half, share)),
        [vmem],
        (vmem, vmem),
    )(landed)
    weight_grad = exchange(spread, same_core).reshape(size, width)
    return (output, weight_grad, feature_grad)


def solution(mesh):
    return jax.shard_map(
        on_device,
        mesh=mesh,
        in_specs=(
            P(("row", "col", "depth"), None),
            P(),
            P("row", "col", "depth", None, None, None),
            P("row", "col", "depth", None),
            P("row", "col", "depth"),
            P(("row", "col", "depth"), None),
        ),
        out_specs=(P(("row", "col", "depth"), None), P(), P(("row", "col", "depth"), None)),
        check_vma=False,
    )
```

```python
import functools
import math

import jax
import jax.numpy as jnp
from jax import lax
from jax.experimental import pallas as pl
from jax.experimental.pallas import tpu as pltpu
from jax.sharding import PartitionSpec as P

MEM = 48 * 1024 * 1024
TURN = 8
CD = ("col", "depth")


def split_bf16(value):
    high = value.astype(jnp.bfloat16)
    low = (value - high.astype(jnp.float32)).astype(jnp.bfloat16)
    return high, low


def dot3(left, right, dims):
    lh, ll = split_bf16(left)
    rh, rl = split_bf16(right)

    def one(a, b):
        return lax.dot_general(a, b, (dims, ((), ())), preferred_element_type=jnp.float32)

    return one(lh, rh) + (one(lh, rl) + one(ll, rh))


def turned(at):
    return at ^ (at // 2)


def half_place(block, inner, outer):
    half, run, step = (block // inner) % 2, block // (2 * inner), block % inner
    run = turned(run)
    step = turned(step)
    depth_first = step * outer + run
    return half, jnp.where(half == 0, depth_first, run * inner + step)


def tile_product(tile, data, transposed):
    high, low = split_bf16(data)
    axis = 0 if transposed else 1
    return lax.dot_general(
        jnp.concatenate([tile, tile], axis=axis),
        jnp.concatenate([high, low], axis=0),
        (((axis,), (0,)), ((), ())),
        preferred_element_type=jnp.float32,
    )


def parity_place(block):
    return block % 2, ((block % TURN) // 2) * 2 + block // TURN


def forward_kernel(inner, outer, blocks, index_ref, count_ref, tiles_ref, near_ref, far_ref, keep_ref, send_ref):
    core = lax.axis_index("col") % 2
    mine = lax.axis_index("row") % 2
    keep_ref[...] = jnp.zeros_like(keep_ref)
    send_ref[...] = jnp.zeros_like(send_ref)
    for slot in range(tiles_ref.shape[0]):
        place = index_ref[slot]
        half, spot = half_place(place // blocks, inner, outer)
        parity, at = parity_place(place % blocks)
        data = jnp.where(parity == mine, near_ref[at], far_ref[at])
        data = jnp.where(slot < count_ref[0], data, 0.0)
        product = tile_product(tiles_ref[slot], data, False)
        kept = half == core
        keep_ref[spot] = keep_ref[spot] + jnp.where(kept, product, 0.0)
        send_ref[spot] = send_ref[spot] + jnp.where(kept, 0.0, product)


def middle_kernel(inner, parts_ref, weight_ref, cot_ref, output_ref, packet_ref):
    core = lax.axis_index("col") % 2
    total = parts_ref[0]
    for peer in range(1, parts_ref.shape[0]):
        total = total + parts_ref[peer]
    weight = weight_ref[...]
    pre = dot3(total, weight, ((1,), (0,)))
    sig = jax.nn.sigmoid(pre)
    output_ref[...] = pre * sig
    grad = cot_ref[...] * sig * (1.0 + pre * (1.0 - sig))
    moving = dot3(grad, weight, ((1,), (1,)))
    term = dot3(total, grad, ((0,), (0,)))
    size = moving.shape[0]
    peers = packet_ref.shape[0]
    rows = size // (peers * inner)
    for peer in range(peers):
        packet_ref[peer, 0:size] = moving
        for step in range(inner):
            at = (peer * inner + step) * rows
            piece = term[at : at + rows]
            at = (step * inner + peer) * rows
            piece = jnp.where(core == 0, piece, term[at : at + rows])
            packet_ref[peer, size + step * rows : size + (step + 1) * rows] = piece


def repack_kernel(landed_ref, packet_ref):
    outer, length = landed_ref.shape[0], landed_ref.shape[1]
    part, size = packet_ref.shape[1], landed_ref.shape[2]
    term = landed_ref[0, size:length]
    for peer in range(1, outer):
        term = term + landed_ref[peer, size:length]
    share = part - outer * size
    for peer in range(packet_ref.shape[0]):
        for piece in range(outer):
            packet_ref[peer, piece * size : (piece + 1) * size] = landed_ref[piece, 0:size]
        packet_ref[peer, outer * size : part] = term[peer * share : (peer + 1) * share]


def backward_kernel(
    inner, outer, blocks, index_ref, count_ref, tiles_ref, own_ref, other_ref, keep_ref, away_ref
):
    size = tiles_ref.shape[1]
    core = lax.axis_index("col") % 2
    mine = lax.axis_index("row") % 2
    span = outer * size
    term = own_ref[0, span:] + other_ref[0, span:]
    for peer in range(1, own_ref.shape[0]):
        term = term + (own_ref[peer, span:] + other_ref[peer, span:])
    zero = jnp.zeros((size, keep_ref.shape[2]), jnp.float32)
    for block in range(keep_ref.shape[0]):
        for ref in (keep_ref, away_ref):
            ref[block, 0:size] = zero
            ref[block, size:] = term
    for slot in range(tiles_ref.shape[0]):
        place = index_ref[slot]
        half, spot = half_place(place // blocks, inner, outer)
        parity, to = parity_place(place % blocks)
        at = pl.ds(pl.multiple_of((spot % outer) * size, size), size)
        data = jnp.where(half == core, own_ref[spot // outer, at], other_ref[spot // outer, at])
        data = jnp.where(slot < count_ref[0], data, 0.0)
        product = tile_product(tiles_ref[slot], data, True)
        kept = parity == mine
        keep_ref[to, 0:size] = keep_ref[to, 0:size] + jnp.where(kept, product, 0.0)
        away_ref[to, 0:size] = away_ref[to, 0:size] + jnp.where(kept, 0.0, product)


def last_kernel(scale, landed_ref, grad_ref, spread_ref):
    size = grad_ref.shape[0]
    total = landed_ref[0]
    for peer in range(1, landed_ref.shape[0]):
        total = total + landed_ref[peer]
    grad_ref[...] = total[0:size]
    for peer in range(spread_ref.shape[0]):
        spread_ref[peer] = total[size:] * scale


def on_device(features, weight, tile_values, tile_index, tile_counts, cotangent):
    tiles = tile_values.reshape(tile_values.shape[-3:])
    slot_index = tile_index.reshape(-1)
    live_count = tile_counts.reshape(-1)
    size, width = features.shape
    rows = lax.axis_size("row")
    cols = lax.axis_size("col")
    inner = lax.axis_size("depth")
    outer = cols // 2
    assert inner == outer
    half = outer * inner
    share = size // half
    node_total = size * rows * cols * inner
    swap = [(i, i ^ 1) for i in range(cols)]
    place = lambda z, c, x: (z * 2 + c) * inner + x
    along_depth = [[[place(z, c, x) for x in map(turned, range(inner))] for z in map(turned, range(outer))] for c in range(2)]
    along_col = [[[place(z, c, x) for z in map(turned, range(outer))] for x in map(turned, range(inner))] for c in range(2)]
    large, small = along_depth[0] + along_col[1], along_col[0] + along_depth[1]
    def beside(row, core):
        base, y = row - row % TURN, row % TURN
        return base + (y + (1 if (y + core) % 2 == 0 else -1)) % TURN

    same_parity = [[z + y for y in range(p, TURN, 2) for z in range(0, rows, TURN)] for p in range(2)]
    neighbour = [(y * cols + c, beside(y, c % 2) * cols + c) for y in range(rows) for c in range(cols)]
    same_core = [[place(z, c, x) for z in map(turned, range(outer)) for x in map(turned, range(inner))] for c in range(2)]
    smem = pl.BlockSpec(memory_space=pltpu.SMEM)
    vmem = pl.BlockSpec(memory_space=pltpu.VMEM)

    def shape(*dims):
        return jax.ShapeDtypeStruct(dims + (width,), jnp.float32)

    def call(kernel, name, out_shape, in_specs, out_specs, scratch=()):
        return pl.pallas_call(
            kernel,
            out_shape=out_shape,
            in_specs=in_specs,
            out_specs=out_specs,
            scratch_shapes=scratch,
            compiler_params=pltpu.CompilerParams(vmem_limit_bytes=MEM),
            name=name,
        )

    def exchange(value, groups):
        return lax.all_to_all(value, CD, 0, 0, tiled=True, axis_index_groups=groups)

    spread = jnp.broadcast_to(features[None], (rows // 2, size, width))
    near = lax.all_to_all(spread, "row", 0, 0, tiled=True, axis_index_groups=same_parity)
    far = lax.ppermute(near, ("row", "col"), neighbour)
    keep, send = call(
        functools.partial(forward_kernel, inner, outer, rows),
        "forward_tiles",
        (shape(half, size), shape(half, size)),
        [smem, smem, vmem, vmem, vmem],
        (vmem, vmem),
    )(slot_index, live_count, tiles, near, far)
    parts = keep + lax.ppermute(send, "col", swap)
    landed = exchange(parts.reshape(inner, outer * size, width), large)
    parts = exchange(landed.sum(axis=0).reshape(outer, size, width), small)
    output, packet = call(
        functools.partial(middle_kernel, inner),
        "dense_layer",
        (shape(size), shape(outer, size + size // outer)),
        [vmem, vmem, vmem],
        (vmem, vmem),
    )(parts, weight, cotangent)
    landed = exchange(packet, small)
    packet = call(repack_kernel, "repack", shape(inner, outer * size + share), [vmem], vmem)(landed)
    own = exchange(packet, large)
    other = lax.ppermute(own, "col", swap)
    keep, away = call(
        functools.partial(backward_kernel, inner, outer, rows),
        "backward_tiles",
        (shape(rows // 2, size + share),) * 2,
        [smem, smem, vmem, vmem, vmem],
        (vmem, vmem),
    )(slot_index, live_count, tiles, own, other)
    moved = keep + lax.ppermute(away, ("row", "col"), neighbour)
    landed = lax.all_to_all(moved, "row", 0, 0, tiled=True, axis_index_groups=same_parity)
    feature_grad, spread = call(
        functools.partial(last_kernel, 1.0 / math.sqrt(node_total)),
        "add_landed",
        (shape(size), shape(half, share)),
        [vmem],
        (vmem, vmem),
    )(landed)
    weight_grad = exchange(spread, same_core).reshape(size, width)
    return (output, weight_grad, feature_grad)


def solution(mesh):
    return jax.shard_map(
        on_device,
        mesh=mesh,
        in_specs=(
            P(("row", "col", "depth"), None),
            P(),
            P("row", "col", "depth", None, None, None),
            P("row", "col", "depth", None),
            P("row", "col", "depth"),
            P(("row", "col", "depth"), None),
        ),
        out_specs=(P(("row", "col", "depth"), None), P(), P(("row", "col", "depth"), None)),
        check_vma=False,
    )
```

```python
import functools
import math

import jax
import jax.numpy as jnp
from jax import lax
from jax.experimental import pallas as pl
from jax.experimental.pallas import tpu as pltpu
from jax.sharding import PartitionSpec as P

MEM = 48 * 1024 * 1024
TURN = 8
CD = ("col", "depth")


def split_bf16(value):
    high = value.astype(jnp.bfloat16)
    low = (value - high.astype(jnp.float32)).astype(jnp.bfloat16)
    return high, low


def dot3(left, right, dims):
    lh, ll = split_bf16(left)
    rh, rl = split_bf16(right)

    def one(a, b):
        return lax.dot_general(a, b, (dims, ((), ())), preferred_element_type=jnp.float32)

    return one(lh, rh) + (one(lh, rl) + one(ll, rh))


def turned(at):
    return at ^ (at // 2)


def half_place(block, inner, outer):
    half, run, step = (block // inner) % 2, block // (2 * inner), block % inner
    run = turned(run)
    step = turned(step)
    depth_first = step * outer + run
    return half, jnp.where(half == 0, depth_first, run * inner + step)


def tile_product(tile, data, transposed):
    high, low = split_bf16(data)
    axis = 0 if transposed else 1
    return lax.dot_general(
        jnp.concatenate([tile, tile], axis=axis),
        jnp.concatenate([high, low], axis=0),
        (((axis,), (0,)), ((), ())),
        preferred_element_type=jnp.float32,
    )


def parity_place(block):
    return block % 2, ((block % TURN) // 2) * 2 + block // TURN


def forward_kernel(inner, outer, blocks, index_ref, count_ref, tiles_ref, near_ref, far_ref, keep_ref, send_ref, prod_ref):
    core = lax.axis_index("col") % 2
    mine = lax.axis_index("row") % 2
    keep_ref[...] = jnp.zeros_like(keep_ref)
    send_ref[...] = jnp.zeros_like(send_ref)
    for slot in range(tiles_ref.shape[0]):
        place = index_ref[slot]
        half, spot = half_place(place // blocks, inner, outer)
        parity, at = parity_place(place % blocks)
        data = jnp.where(parity == mine, near_ref[at], far_ref[at])
        data = jnp.where(slot < count_ref[0], data, 0.0)
        prod_ref[slot] = tile_product(tiles_ref[slot], data, False)
    for slot in range(tiles_ref.shape[0]):
        half, spot = half_place(index_ref[slot] // blocks, inner, outer)
        product = prod_ref[slot]
        kept = half == core
        keep_ref[spot] = keep_ref[spot] + jnp.where(kept, product, 0.0)
        send_ref[spot] = send_ref[spot] + jnp.where(kept, 0.0, product)


def middle_kernel(inner, parts_ref, weight_ref, cot_ref, output_ref, packet_ref):
    core = lax.axis_index("col") % 2
    total = parts_ref[0]
    for peer in range(1, parts_ref.shape[0]):
        total = total + parts_ref[peer]
    weight = weight_ref[...]
    pre = dot3(total, weight, ((1,), (0,)))
    sig = jax.nn.sigmoid(pre)
    output_ref[...] = pre * sig
    grad = cot_ref[...] * sig * (1.0 + pre * (1.0 - sig))
    moving = dot3(grad, weight, ((1,), (1,)))
    term = dot3(total, grad, ((0,), (0,)))
    size = moving.shape[0]
    peers = packet_ref.shape[0]
    rows = size // (peers * inner)
    for peer in range(peers):
        packet_ref[peer, 0:size] = moving
        for step in range(inner):
            at = (peer * inner + step) * rows
            piece = term[at : at + rows]
            at = (step * inner + peer) * rows
            piece = jnp.where(core == 0, piece, term[at : at + rows])
            packet_ref[peer, size + step * rows : size + (step + 1) * rows] = piece


def repack_kernel(landed_ref, packet_ref):
    outer, length = landed_ref.shape[0], landed_ref.shape[1]
    part, size = packet_ref.shape[1], landed_ref.shape[2]
    term = landed_ref[0, size:length]
    for peer in range(1, outer):
        term = term + landed_ref[peer, size:length]
    share = part - outer * size
    for peer in range(packet_ref.shape[0]):
        for piece in range(outer):
            packet_ref[peer, piece * size : (piece + 1) * size] = landed_ref[piece, 0:size]
        packet_ref[peer, outer * size : part] = term[peer * share : (peer + 1) * share]


def backward_kernel(
    inner, outer, blocks, index_ref, count_ref, tiles_ref, own_ref, other_ref, keep_ref, away_ref, prod_ref
):
    size = tiles_ref.shape[1]
    core = lax.axis_index("col") % 2
    mine = lax.axis_index("row") % 2
    span = outer * size
    term = own_ref[0, span:] + other_ref[0, span:]
    for peer in range(1, own_ref.shape[0]):
        term = term + (own_ref[peer, span:] + other_ref[peer, span:])
    zero = jnp.zeros((size, keep_ref.shape[2]), jnp.float32)
    for block in range(keep_ref.shape[0]):
        for ref in (keep_ref, away_ref):
            ref[block, 0:size] = zero
            ref[block, size:] = term
    for slot in range(tiles_ref.shape[0]):
        place = index_ref[slot]
        half, spot = half_place(place // blocks, inner, outer)
        at = pl.ds(pl.multiple_of((spot % outer) * size, size), size)
        data = jnp.where(half == core, own_ref[spot // outer, at], other_ref[spot // outer, at])
        data = jnp.where(slot < count_ref[0], data, 0.0)
        prod_ref[slot] = tile_product(tiles_ref[slot], data, True)
    for slot in range(tiles_ref.shape[0]):
        parity, to = parity_place(index_ref[slot] % blocks)
        product = prod_ref[slot]
        kept = parity == mine
        keep_ref[to, 0:size] = keep_ref[to, 0:size] + jnp.where(kept, product, 0.0)
        away_ref[to, 0:size] = away_ref[to, 0:size] + jnp.where(kept, 0.0, product)


def last_kernel(scale, landed_ref, grad_ref, spread_ref):
    size = grad_ref.shape[0]
    total = landed_ref[0]
    for peer in range(1, landed_ref.shape[0]):
        total = total + landed_ref[peer]
    grad_ref[...] = total[0:size]
    for peer in range(spread_ref.shape[0]):
        spread_ref[peer] = total[size:] * scale


def on_device(features, weight, tile_values, tile_index, tile_counts, cotangent):
    tiles = tile_values.reshape(tile_values.shape[-3:])
    slot_index = tile_index.reshape(-1)
    live_count = tile_counts.reshape(-1)
    capacity = tiles.shape[0]
    size, width = features.shape
    rows = lax.axis_size("row")
    cols = lax.axis_size("col")
    inner = lax.axis_size("depth")
    outer = cols // 2
    assert inner == outer
    half = outer * inner
    share = size // half
    node_total = size * rows * cols * inner
    swap = [(i, i ^ 1) for i in range(cols)]
    place = lambda z, c, x: (z * 2 + c) * inner + x
    along_depth = [[[place(z, c, x) for x in map(turned, range(inner))] for z in map(turned, range(outer))] for c in range(2)]
    along_col = [[[place(z, c, x) for z in map(turned, range(outer))] for x in map(turned, range(inner))] for c in range(2)]
    large, small = along_depth[0] + along_col[1], along_col[0] + along_depth[1]
    def beside(row, core):
        base, y = row - row % TURN, row % TURN
        return base + (y + (1 if (y + core) % 2 == 0 else -1)) % TURN

    same_parity = [[z + y for y in range(p, TURN, 2) for z in range(0, rows, TURN)] for p in range(2)]
    neighbour = [(y * cols + c, beside(y, c % 2) * cols + c) for y in range(rows) for c in range(cols)]
    same_core = [[place(z, c, x) for z in map(turned, range(outer)) for x in map(turned, range(inner))] for c in range(2)]
    smem = pl.BlockSpec(memory_space=pltpu.SMEM)
    vmem = pl.BlockSpec(memory_space=pltpu.VMEM)

    def shape(*dims):
        return jax.ShapeDtypeStruct(dims + (width,), jnp.float32)

    def call(kernel, name, out_shape, in_specs, out_specs, scratch=()):
        return pl.pallas_call(
            kernel,
            out_shape=out_shape,
            in_specs=in_specs,
            out_specs=out_specs,
            scratch_shapes=scratch,
            compiler_params=pltpu.CompilerParams(vmem_limit_bytes=MEM),
            name=name,
        )

    def exchange(value, groups):
        return lax.all_to_all(value, CD, 0, 0, tiled=True, axis_index_groups=groups)

    spread = jnp.broadcast_to(features[None], (rows // 2, size, width))
    near = lax.all_to_all(spread, "row", 0, 0, tiled=True, axis_index_groups=same_parity)
    far = lax.ppermute(near, ("row", "col"), neighbour)
    keep, send = call(
        functools.partial(forward_kernel, inner, outer, rows),
        "forward_tiles",
        (shape(half, size), shape(half, size)),
        [smem, smem, vmem, vmem, vmem],
        (vmem, vmem),
        [pltpu.VMEM((capacity, size, width), jnp.float32)],
    )(slot_index, live_count, tiles, near, far)
    parts = keep + lax.ppermute(send, "col", swap)
    landed = exchange(parts.reshape(inner, outer * size, width), large)
    parts = exchange(landed.sum(axis=0).reshape(outer, size, width), small)
    output, packet = call(
        functools.partial(middle_kernel, inner),
        "dense_layer",
        (shape(size), shape(outer, size + size // outer)),
        [vmem, vmem, vmem],
        (vmem, vmem),
    )(parts, weight, cotangent)
    landed = exchange(packet, small)
    packet = call(repack_kernel, "repack", shape(inner, outer * size + share), [vmem], vmem)(landed)
    own = exchange(packet, large)
    other = lax.ppermute(own, "col", swap)
    keep, away = call(
        functools.partial(backward_kernel, inner, outer, rows),
        "backward_tiles",
        (shape(rows // 2, size + share),) * 2,
        [smem, smem, vmem, vmem, vmem],
        (vmem, vmem),
        [pltpu.VMEM((capacity, size, width), jnp.float32)],
    )(slot_index, live_count, tiles, own, other)
    moved = keep + lax.ppermute(away, ("row", "col"), neighbour)
    landed = lax.all_to_all(moved, "row", 0, 0, tiled=True, axis_index_groups=same_parity)
    feature_grad, spread = call(
        functools.partial(last_kernel, 1.0 / math.sqrt(node_total)),
        "add_landed",
        (shape(size), shape(half, share)),
        [vmem],
        (vmem, vmem),
    )(landed)
    weight_grad = exchange(spread, same_core).reshape(size, width)
    return (output, weight_grad, feature_grad)


def solution(mesh):
    return jax.shard_map(
        on_device,
        mesh=mesh,
        in_specs=(
            P(("row", "col", "depth"), None),
            P(),
            P("row", "col", "depth", None, None, None),
            P("row", "col", "depth", None),
            P("row", "col", "depth"),
            P(("row", "col", "depth"), None),
        ),
        out_specs=(P(("row", "col", "depth"), None), P(), P(("row", "col", "depth"), None)),
        check_vma=False,
    )
```
